32 devices in a mesh: wide: 4 (over z), blk: 4 (over y, x), col: 2 (over core).
Axes of the slice: x: 2, y: 2, z: 4, core: 2. Of those that a mesh axis runs over, the one named last changes fastest.
Arguments:
- tensor: float32 [1536, 64, 512], P(('blk', 'col'), 'wide'), may hold values from -6 to 6
- density: float32 [1536, 1536], P(('blk', 'col'), 'wide'), may hold values from -0.21875 to 0.21875
- tensor_mask: int32 [24, 8], replicated, may hold values 0 or 1
- density_mask: int32 [24, 24], replicated, may hold values 0 or 1
Outputs:
- contracted: float32 [1536, 64, 512], P(('blk', 'col'), 'wide')
The draws below stay inside these ranges and needn't reach their ends.
All inputs are finite; a program needn't handle non-finite values.
Results may differ from the reference program's by a relative error of at most 0.00007.
Values sent between devices are 32-bit elements; how exact they have to be, the bound alone decides.
A program may use at most 128 MiB of HBM per device.

```python
import jax
import jax.numpy as jnp
from jax import lax

BS = 64
RI = 64
NMB = 24
NMU = 1536
NUB = 24
NU = 1536
NLB = 8
NLAM = 512


def touch_ends(array, own_key, low, top_value):
    dims = array.shape
    place = [jax.random.randint(jax.random.fold_in(own_key, axis), (), 0, dims[axis]) for axis in range(len(dims))]
    array = array.at[tuple(place)].set(low)
    longest = dims.index(max(dims))
    place[longest] = (place[longest] + 1) % dims[longest]
    return array.at[tuple(place)].set(top_value)


def levels(own_key, extent, split, smallest, top_value):
    factor_of, own = 1.0, jax.random.fold_in(own_key, 6)
    for axis_at, parts in split:
        steps = jnp.exp(jax.random.uniform(jax.random.fold_in(own, axis_at), (parts,), jnp.float32, smallest / len(split), top_value / len(split)))
        factor_of = factor_of * jnp.repeat(steps, extent[axis_at] // parts).reshape([-1 if axis == axis_at else 1 for axis in range(len(extent))])
    return factor_of


def scatter_about(rng, extent, scale, most, split=(), dtype=jnp.bfloat16):
    result = jax.random.normal(rng, extent, jnp.float32) * scale
    if len(split) > 0:
        result = levels(rng, extent, split, -0.22, 0.18) * result
    return jnp.clip(result, min=-most, max=most).astype(dtype)


def setup_inputs(seed: int = 0) -> dict:
    arg_keys = jax.random.split(jax.random.key(seed), 5)
    tensor = scatter_about(arg_keys[0], (NMU, RI, NLAM), 1.0, 6.0, ((0, 8), (1, 4)), jnp.float32)
    density = scatter_about(arg_keys[1], (NU, NMU), (NMU // 2) ** -0.5, 0.21875, ((0, 8), (1, 4)), jnp.float32)
    tensor_mask = touch_ends((jax.random.randint(arg_keys[2], (NMB, NLB), 0, 3) < 2).astype(jnp.int32), jax.random.fold_in(arg_keys[2], 1), 0, 1)
    density_mask = touch_ends((jax.random.randint(arg_keys[3], (NUB, NMB), 0, 2) < 1).astype(jnp.int32), jax.random.fold_in(arg_keys[3], 1), 0, 1)
    return {"tensor": tensor, "density": density, "tensor_mask": tensor_mask, "density_mask": density_mask}


def reference(tensor, density, tensor_mask, density_mask):
    t_keep = jnp.repeat(jnp.repeat(tensor_mask, BS, axis=0), BS, axis=1).astype(jnp.float32)
    screened = tensor * t_keep[:, None, :]
    d_keep = jnp.repeat(jnp.repeat(density_mask, BS, axis=0), BS, axis=1).astype(jnp.float32)
    kept = density * d_keep
    product = jnp.dot(kept, screened.reshape(NMU, RI * NLAM), precision=lax.Precision.HIGHEST, preferred_element_type=jnp.float32)
    return product.reshape(NU, RI, NLAM)
```

```python
import functools

import jax
import jax.numpy as jnp
from jax import lax
from jax.experimental import pallas as pl
from jax.experimental.pallas import tpu as pltpu
from jax.sharding import PartitionSpec as P

BS = 64
LANES = 512
MESH = pl.DeviceIdType.MESH


def other_blk(b, h):
    if h == 0:
        return b + 1 - 2 * lax.rem(b, 2)
    return lax.rem(b + 2, 4)


def kernel(
    spread, wide, ri, nl,
    t_hbm, d_ref, tm_ref, o_hbm,
    T, X, Pown, Psend, Precv, D, DL, th, tl,
    load_sem, s_ici, r_ici, s_core, r_core, s_fwd, r_fwd, s_p, r_p, o_sem, s_dn, s_dz, r_d,
):
    Q = ri * nl
    half = Q // 2
    mu = T.shape[2]
    b = lax.axis_index("blk")
    c = lax.axis_index("col")
    w = lax.axis_index("wide")
    nbr = [other_blk(b, 0), other_blk(b, 1)]
    diag = other_blk(nbr[0], 1)

    def hbm_view(ref, q):
        return ref.at[:, q // nl, pl.ds(pl.multiple_of(lax.rem(q, nl) * LANES, LANES), LANES)]

    def load(q):
        return pltpu.make_async_copy(hbm_view(t_hbm, q), T.at[c, q], load_sem.at[q])

    def remote(src, dst, ss, rs, dev):
        return pltpu.make_async_remote_copy(
            src_ref=src, dst_ref=dst, send_sem=ss, recv_sem=rs, device_id=dev, device_id_type=MESH
        )

    def send_ici(q, h):
        return remote(T.at[c, q], X.at[c, q], s_ici.at[q], r_ici.at[q], {"blk": nbr[h]})

    def send_core(q):
        return remote(T.at[c, q], T.at[c, q], s_core.at[q], r_core.at[q], {"col": 1 - c})

    def recv_core(q):
        return remote(T.at[c, q], T.at[1 - c, q], s_core.at[q], r_core.at[q], {"col": 1 - c})

    def send_fwd(q):
        return remote(X.at[c, q], X.at[c, q], s_fwd.at[q], r_fwd.at[q], {"col": 1 - c})

    def recv_fwd(q):
        return remote(X.at[c, q], X.at[1 - c, q], s_fwd.at[q], r_fwd.at[q], {"col": 1 - c})

    def send_p(q, h):
        return remote(Psend.at[q], Precv.at[q], s_p.at[q], r_p.at[q], {"blk": nbr[1 - h]})

    def store_out(q):
        return pltpu.make_async_copy(Pown.at[q], hbm_view(o_hbm, q), o_sem.at[q])

    def start_load(q, _):
        load(q).start()
        return 0

    lax.fori_loop(0, Q, start_load, 0)

    barrier = pltpu.get_barrier_semaphore()
    count = 3
    for h in range(2):
        pl.semaphore_signal(barrier, inc=1, device_id={"blk": nbr[h]}, device_id_type=MESH)
    pl.semaphore_signal(barrier, inc=1, device_id={"col": 1 - c}, device_id_type=MESH)
    if spread:
        for o in range(1, wide):
            pl.semaphore_signal(
                barrier, inc=1, device_id={"wide": lax.rem(w + o, wide)}, device_id_type=MESH
            )
        count += wide - 1
        D[0, w] = d_ref[...]
    else:
        D[...] = d_ref[...]
    pl.semaphore_wait(barrier, count)

    def need_own(m):
        return m != diag

    def need_0(m):
        return lax.rem(m, 2) == lax.rem(b, 2)

    def need_1(m):
        return m // 2 == b // 2

    needs = [need_own, need_0, need_1]

    def d_to_nbr(h):
        return remote(D.at[0, w], D.at[1 + h, w], s_dn.at[h], r_d.at[1 + h, w], {"blk": nbr[h]})

    def d_spread(r, o):
        dev = {"wide": lax.rem(w + o, wide)}
        return remote(D.at[r, w], D.at[r, w], s_dz.at[r, o], r_d.at[r, w], dev)

    def d_arrive(r, m):
        return remote(D.at[r, m], D.at[r, m], s_dz.at[r, 0], r_d.at[r, m], {"wide": lax.rem(w + 1, wide)})

    if spread:
        gives = [lax.rem(w, 2) != lax.rem(b, 2), w // 2 != b // 2]
        for h in range(2):
            @pl.when(gives[h])
            def _():
                d_to_nbr(h).start()

        @pl.when(need_own(w))
        def _():
            for o in range(1, wide):
                d_spread(0, o).start()

    def issue(k, _):
        for h in range(2):
            q = h * half + k
            load(q).wait()
            T[c, q] = T[c, q] * tm_ref[lax.rem(q, nl)]
            send_ici(q, h).start()
            send_core(q).start()
        return 0

    lax.fori_loop(0, half, issue, 0)

    if spread:
        for r in (1, 2):
            @pl.when(needs[r](w))
            def _():
                d_arrive(r, w).wait_recv()
                for o in range(1, wide):
                    d_spread(r, o).start()
        for r in range(3):
            for o in range(1, wide):
                m = lax.rem(w + o, wide)

                @pl.when(needs[r](m))
                def _():
                    d_arrive(r, m).wait_recv()

    kd = D.shape[3]
    for h in range(2):
        for i, r in enumerate((0, 2 - h)):
            for j, m in enumerate((b, nbr[h])):
                block = D[r, m]
                hi = block.astype(jnp.bfloat16)
                lo = (block - hi.astype(jnp.float32)).astype(jnp.bfloat16)
                DL[h, i * mu:(i + 1) * mu, j * kd:(j + 1) * kd] = hi
                DL[h, (2 + i) * mu:(3 + i) * mu, j * kd:(j + 1) * kd] = lo

    def forward(k):
        for h in range(2):
            q = h * half + k
            send_ici(q, h).wait_recv()
            send_fwd(q).start()

    def compute(k, _):
        forward(k)
        for h in range(2):
            q = h * half + k
            recv_core(q).wait_recv()
            recv_fwd(q).wait_recv()
            for i in range(4):
                piece = T[i, q] if i < 2 else X[i - 2, q]
                hi = piece.astype(jnp.bfloat16)
                th[i * mu:(i + 1) * mu] = hi
                tl[i * mu:(i + 1) * mu] = (piece - hi.astype(jnp.float32)).astype(jnp.bfloat16)
            first = jnp.dot(DL[h], th[...], preferred_element_type=jnp.float32)
            second = jnp.dot(DL[h, :2 * mu], tl[...], preferred_element_type=jnp.float32)
            total = first[:2 * mu] + first[2 * mu:] + second
            Psend[q] = total[mu:]
            send_p(q, h).start()
            Pown[q] = total[:mu]
        return 0

    lax.fori_loop(0, half, compute, 0)

    def finish(k, _):
        for h in range(2):
            q = h * half + k
            send_p(q, h).wait_recv()
            Pown[q] = Pown[q] + Precv[q]
            store_out(q).start()
        return 0

    lax.fori_loop(0, half, finish, 0)

    def drain(k, _):
        for h in range(2):
            q = h * half + k
            send_ici(q, h).wait_send()
            send_core(q).wait_send()
            send_fwd(q).wait_send()
            send_p(q, h).wait_send()
            store_out(q).wait()
        return 0

    lax.fori_loop(0, half, drain, 0)

    if spread:
        for h in range(2):
            @pl.when(gives[h])
            def _():
                d_to_nbr(h).wait_send()
        for r in range(3):
            @pl.when(needs[r](w))
            def _():
                for o in range(1, wide):
                    d_spread(r, o).wait_send()


def on_device(tensor, density, tensor_mask, density_mask):
    wide, blk, col = (lax.axis_size(a) for a in ("wide", "blk", "col"))
    mu, ri, lam = tensor.shape
    nu, piece = density.shape
    nl = lam // LANES
    Q = ri * nl
    b, w = lax.axis_index("blk"), lax.axis_index("wide")
    g = b * col + lax.axis_index("col")
    rows = lax.dynamic_slice_in_dim(tensor_mask, g * (mu // BS), mu // BS, 0)
    tm = jnp.repeat(jnp.repeat(rows, BS, axis=0), BS, axis=1).astype(jnp.float32)
    tm = tm.reshape(mu, nl, LANES).transpose(1, 0, 2)
    kd = col * mu
    spread = piece == kd and wide == blk
    dm = jnp.repeat(jnp.repeat(density_mask, BS, axis=0), BS, axis=1).astype(jnp.float32)
    kept = density * lax.dynamic_slice(dm, (g * nu, w * piece), (nu, piece))
    if not spread:
        full = lax.all_gather(kept, "wide", axis=1, tiled=True)
        full = lax.all_gather(full, ("blk", "col"), axis=0, tiled=True)
        groups = [g, other_blk(b, 0) * col + lax.axis_index("col"), other_blk(b, 1) * col + lax.axis_index("col")]
        kept = jnp.stack(
            [lax.dynamic_slice_in_dim(full, i * nu, nu, 0).reshape(nu, blk, kd).transpose(1, 0, 2) for i in groups]
        )
    f32, bf16 = jnp.float32, jnp.bfloat16
    dma = pltpu.SemaphoreType.DMA
    flops = 2 * 2 * nu * 2 * kd * Q * LANES * 3
    return pl.pallas_call(
        functools.partial(kernel, spread, wide, ri, nl),
        out_shape=jax.ShapeDtypeStruct((mu, ri, lam), f32),
        in_specs=[
            pl.BlockSpec(memory_space=pl.ANY),
            pl.BlockSpec(memory_space=pltpu.VMEM),
            pl.BlockSpec(memory_space=pltpu.VMEM),
        ],
        out_specs=pl.BlockSpec(memory_space=pl.ANY),
        scratch_shapes=[
            pltpu.VMEM((2, Q, mu, LANES), f32),
            pltpu.VMEM((2, Q, mu, LANES), f32),
            pltpu.VMEM((Q, nu, LANES), f32),
            pltpu.VMEM((Q, nu, LANES), f32),
            pltpu.VMEM((Q, nu, LANES), f32),
            pltpu.VMEM((3, blk, nu, kd), f32),
            pltpu.VMEM((2, 4 * nu, 2 * kd), bf16),
            pltpu.VMEM((2 * kd, LANES), bf16),
            pltpu.VMEM((2 * kd, LANES), bf16),
        ] + [dma((Q,))] * 10 + [dma((2,)), dma((3, wide)), dma((3, blk))],
        compiler_params=pltpu.CompilerParams(
            collective_id=0, has_side_effects=True, vmem_limit_bytes=62 * 2**20
        ),
        cost_estimate=pl.CostEstimate(
            flops=flops, bytes_accessed=2 * mu * ri * lam * 4, transcendentals=0
        ),
    )(tensor, kept, tm)


def solution(mesh):
    in_specs = (P(("blk", "col"), "wide", None), P(("blk", "col"), "wide"), P(), P())
    out_specs = P(("blk", "col"), "wide", None)
    return jax.shard_map(
        on_device, mesh=mesh, in_specs=in_specs, out_specs=out_specs, check_vma=False
    )
```

```python
import functools

import jax
import jax.numpy as jnp
from jax import lax
from jax.experimental import pallas as pl
from jax.experimental.pallas import tpu as pltpu
from jax.sharding import PartitionSpec as P

BS = 64
LANES = 512
MESH = pl.DeviceIdType.MESH


def other_blk(b, h):
    if h == 0:
        return b + 1 - 2 * lax.rem(b, 2)
    return lax.rem(b + 2, 4)


def kernel(
    spread, wide, ri, nl,
    t_hbm, d_ref, tmask_ref, dmask_ref, o_hbm,
    tm_ref, T, X, Pown, Psend, Precv, D, DL, th, tl,
    load_sem, s_ici, r_ici, s_core, r_core, s_fwd, r_fwd, s_p, r_p, o_sem, s_dn, s_dz, r_d,
):
    Q = ri * nl
    half = Q // 2
    mu = T.shape[2]
    b = lax.axis_index("blk")
    c = lax.axis_index("col")
    w = lax.axis_index("wide")
    g = b * 2 + c
    nbr = [other_blk(b, 0), other_blk(b, 1)]
    diag = other_blk(nbr[0], 1)

    def hbm_view(ref, q):
        return ref.at[:, q // nl, pl.ds(pl.multiple_of(lax.rem(q, nl) * LANES, LANES), LANES)]

    def load(q):
        return pltpu.make_async_copy(hbm_view(t_hbm, q), T.at[c, q], load_sem.at[q])

    def remote(src, dst, ss, rs, dev):
        return pltpu.make_async_remote_copy(
            src_ref=src, dst_ref=dst, send_sem=ss, recv_sem=rs, device_id=dev, device_id_type=MESH
        )

    def send_ici(q, h):
        return remote(T.at[c, q], X.at[c, q], s_ici.at[q], r_ici.at[q], {"blk": nbr[h]})

    def send_core(q):
        return remote(T.at[c, q], T.at[c, q], s_core.at[q], r_core.at[q], {"col": 1 - c})

    def recv_core(q):
        return remote(T.at[c, q], T.at[1 - c, q], s_core.at[q], r_core.at[q], {"col": 1 - c})

    def send_fwd(q):
        return remote(X.at[c, q], X.at[c, q], s_fwd.at[q], r_fwd.at[q], {"col": 1 - c})

    def recv_fwd(q):
        return remote(X.at[c, q], X.at[1 - c, q], s_fwd.at[q], r_fwd.at[q], {"col": 1 - c})

    def send_p(q, h):
        return remote(Psend.at[q], Precv.at[q], s_p.at[q], r_p.at[q], {"blk": nbr[1 - h]})

    def store_out(q):
        return pltpu.make_async_copy(Pown.at[q], hbm_view(o_hbm, q), o_sem.at[q])

    def start_load(k, _):
        for h in range(2):
            load(h * half + k).start()
        return 0

    lax.fori_loop(0, half, start_load, 0)

    def spots(shape, axis, first):
        block = (lax.broadcasted_iota(jnp.int32, shape, axis) + first) // BS
        return (block == lax.broadcasted_iota(jnp.int32, shape, 1 - axis)).astype(jnp.float32)

    def expanded(mask_ref, flipped, rows, row0, columns, column0):
        mask = mask_ref[...].astype(jnp.float32)
        over, kept = (1, 0) if flipped else (0, 1)
        by_row = lax.dot_general(
            spots((rows, mask.shape[over]), 0, row0),
            mask,
            (((1,), (over,)), ((), ())),
            preferred_element_type=jnp.float32,
        )
        return jnp.dot(
            by_row, spots((mask.shape[kept], columns), 1, column0), preferred_element_type=jnp.float32
        )

    barrier = pltpu.get_barrier_semaphore()
    count = 3
    for h in range(2):
        pl.semaphore_signal(barrier, inc=1, device_id={"blk": nbr[h]}, device_id_type=MESH)
    pl.semaphore_signal(barrier, inc=1, device_id={"col": 1 - c}, device_id_type=MESH)
    if spread:
        for o in range(1, wide):
            pl.semaphore_signal(
                barrier, inc=1, device_id={"wide": lax.rem(w + o, wide)}, device_id_type=MESH
            )
        count += wide - 1
        keep = expanded(dmask_ref, False, d_ref.shape[0], g * d_ref.shape[0], d_ref.shape[1], w * d_ref.shape[1])
        D[0, w] = d_ref[...] * keep
    else:
        D[...] = d_ref[...]
    for j in range(nl):
        tm_ref[j] = expanded(tmask_ref, True, mu, g * mu, LANES, j * LANES)
    pl.semaphore_wait(barrier, count)

    def need_own(m):
        return m != diag

    def need_0(m):
        return lax.rem(m, 2) == lax.rem(b, 2)

    def need_1(m):
        return m // 2 == b // 2

    needs = [need_own, need_0, need_1]

    def d_to_nbr(h):
        return remote(D.at[0, w], D.at[1 + h, w], s_dn.at[h], r_d.at[1 + h, w], {"blk": nbr[h]})

    def d_spread(r, o):
        dev = {"wide": lax.rem(w + o, wide)}
        return remote(D.at[r, w], D.at[r, w], s_dz.at[r, o], r_d.at[r, w], dev)

    def d_arrive(r, m):
        return remote(D.at[r, m], D.at[r, m], s_dz.at[r, 0], r_d.at[r, m], {"wide": lax.rem(w + 1, wide)})

    if spread:
        gives = [lax.rem(w, 2) != lax.rem(b, 2), w // 2 != b // 2]
        for h in range(2):
            @pl.when(gives[h])
            def _():
                d_to_nbr(h).start()

        @pl.when(need_own(w))
        def _():
            for o in range(1, wide):
                d_spread(0, o).start()

    def issue(k, _):
        for h in range(2):
            q = h * half + k
            load(q).wait()
            T[c, q] = T[c, q] * tm_ref[lax.rem(q, nl)]
            send_ici(q, h).start()
            send_core(q).start()
        return 0

    lax.fori_loop(0, half, issue, 0)

    if spread:
        for r in (1, 2):
            @pl.when(needs[r](w))
            def _():
                d_arrive(r, w).wait_recv()
                for o in range(1, wide):
                    d_spread(r, o).start()
        for r in range(3):
            for o in range(1, wide):
                m = lax.rem(w + o, wide)

                @pl.when(needs[r](m))
                def _():
                    d_arrive(r, m).wait_recv()

    kd = D.shape[3]
    for h in range(2):
        for i, r in enumerate((0, 2 - h)):
            for j, m in enumerate((b, nbr[h])):
                block = D[r, m]
                hi = block.astype(jnp.bfloat16)
                lo = (block - hi.astype(jnp.float32)).astype(jnp.bfloat16)
                DL[h, i * mu:(i + 1) * mu, j * kd:(j + 1) * kd] = hi
                DL[h, (2 + i) * mu:(3 + i) * mu, j * kd:(j + 1) * kd] = lo

    def forward(k):
        for h in range(2):
            q = h * half + k
            send_ici(q, h).wait_recv()
            send_fwd(q).start()

    def compute(k, _):
        forward(k)
        for h in range(2):
            q = h * half + k
            recv_core(q).wait_recv()
            recv_fwd(q).wait_recv()
            for i in range(4):
                piece = T[i, q] if i < 2 else X[i - 2, q]
                hi = piece.astype(jnp.bfloat16)
                th[i * mu:(i + 1) * mu] = hi
                tl[i * mu:(i + 1) * mu] = (piece - hi.astype(jnp.float32)).astype(jnp.bfloat16)
            first = jnp.dot(DL[h], th[...], preferred_element_type=jnp.float32)
            second = jnp.dot(DL[h, :2 * mu], tl[...], preferred_element_type=jnp.float32)
            total = first[:2 * mu] + first[2 * mu:] + second
            Psend[q] = total[mu:]
            send_p(q, h).start()
            Pown[q] = total[:mu]
        return 0

    lax.fori_loop(0, half, compute, 0)

    def finish(k, _):
        for h in range(2):
            q = h * half + k
            send_p(q, h).wait_recv()
            Pown[q] = Pown[q] + Precv[q]
            store_out(q).start()
        return 0

    lax.fori_loop(0, half, finish, 0)

    def drain(k, _):
        for h in range(2):
            q = h * half + k
            send_ici(q, h).wait_send()
            send_core(q).wait_send()
            send_fwd(q).wait_send()
            send_p(q, h).wait_send()
            store_out(q).wait()
        return 0

    lax.fori_loop(0, half, drain, 0)

    if spread:
        for h in range(2):
            @pl.when(gives[h])
            def _():
                d_to_nbr(h).wait_send()
        for r in range(3):
            @pl.when(needs[r](w))
            def _():
                for o in range(1, wide):
                    d_spread(r, o).wait_send()


def on_device(tensor, density, tensor_mask, density_mask):
    wide, blk, col = (lax.axis_size(a) for a in ("wide", "blk", "col"))
    mu, ri, lam = tensor.shape
    nu, piece = density.shape
    nl = lam // LANES
    Q = ri * nl
    b, w = lax.axis_index("blk"), lax.axis_index("wide")
    g = b * col + lax.axis_index("col")
    kd = col * mu
    spread = piece == kd and wide == blk
    kept = density
    if not spread:
        dm = jnp.repeat(jnp.repeat(density_mask, BS, axis=0), BS, axis=1).astype(jnp.float32)
        kept = density * lax.dynamic_slice(dm, (g * nu, w * piece), (nu, piece))
        full = lax.all_gather(kept, "wide", axis=1, tiled=True)
        full = lax.all_gather(full, ("blk", "col"), axis=0, tiled=True)
        groups = [g, other_blk(b, 0) * col + lax.axis_index("col"), other_blk(b, 1) * col + lax.axis_index("col")]
        kept = jnp.stack(
            [lax.dynamic_slice_in_dim(full, i * nu, nu, 0).reshape(nu, blk, kd).transpose(1, 0, 2) for i in groups]
        )
    f32, bf16 = jnp.float32, jnp.bfloat16
    dma = pltpu.SemaphoreType.DMA
    flops = 2 * 2 * nu * 2 * kd * Q * LANES * 3
    return pl.pallas_call(
        functools.partial(kernel, spread, wide, ri, nl),
        out_shape=jax.ShapeDtypeStruct((mu, ri, lam), f32),
        in_specs=[
            pl.BlockSpec(memory_space=pl.ANY),
            pl.BlockSpec(memory_space=pltpu.VMEM),
            pl.BlockSpec(memory_space=pltpu.VMEM),
            pl.BlockSpec(memory_space=pltpu.VMEM),
        ],
        out_specs=pl.BlockSpec(memory_space=pl.ANY),
        scratch_shapes=[
            pltpu.VMEM((nl, mu, LANES), f32),
            pltpu.VMEM((2, Q, mu, LANES), f32),
            pltpu.VMEM((2, Q, mu, LANES), f32),
            pltpu.VMEM((Q, nu, LANES), f32),
            pltpu.VMEM((Q, nu, LANES), f32),
            pltpu.VMEM((Q, nu, LANES), f32),
            pltpu.VMEM((3, blk, nu, kd), f32),
            pltpu.VMEM((2, 4 * nu, 2 * kd), bf16),
            pltpu.VMEM((2 * kd, LANES), bf16),
            pltpu.VMEM((2 * kd, LANES), bf16),
        ] + [dma((Q,))] * 10 + [dma((2,)), dma((3, wide)), dma((3, blk))],
        compiler_params=pltpu.CompilerParams(
            collective_id=0, has_side_effects=True, vmem_limit_bytes=62 * 2**20
        ),
        cost_estimate=pl.CostEstimate(
            flops=flops, bytes_accessed=2 * mu * ri * lam * 4, transcendentals=0
        ),
    )(tensor, kept, tensor_mask.T, density_mask)


def solution(mesh):
    in_specs = (P(("blk", "col"), "wide", None), P(("blk", "col"), "wide"), P(), P())
    out_specs = P(("blk", "col"), "wide", None)
    return jax.shard_map(
        on_device, mesh=mesh, in_specs=in_specs, out_specs=out_specs, check_vma=False
    )
```

```python
import functools

import jax
import jax.numpy as jnp
from jax import lax
from jax.experimental import pallas as pl
from jax.experimental.pallas import tpu as pltpu
from jax.sharding import PartitionSpec as P

BS = 64
LANES = 512
MESH = pl.DeviceIdType.MESH


def other_blk(b, h):
    if h == 0:
        return b + 1 - 2 * lax.rem(b, 2)
    return lax.rem(b + 2, 4)


def kernel(
    spread, wide, ri, nl,
    t_hbm, d_hbm, tmask_hbm, dmask_hbm, o_hbm,
    tmask_ref, dmask_ref, tm_ref, T, X, Precv, D, DL, th, tl,
    load_sem, s_ici, r_ici, s_core, r_core, s_fwd, r_fwd, s_p, r_p, o_sem, s_dn, s_dz, r_d, in_sem,
):
    Q = ri * nl
    half = Q // 2
    mu = T.shape[2]
    b = lax.axis_index("blk")
    c = lax.axis_index("col")
    w = lax.axis_index("wide")
    g = b * 2 + c
    nbr = [other_blk(b, 0), other_blk(b, 1)]
    diag = other_blk(nbr[0], 1)

    def hbm_view(ref, q):
        return ref.at[:, q // nl, pl.ds(pl.multiple_of(lax.rem(q, nl) * LANES, LANES), LANES)]

    def load(q):
        return pltpu.make_async_copy(hbm_view(t_hbm, q), T.at[c, q], load_sem.at[q])

    def remote(src, dst, ss, rs, dev):
        return pltpu.make_async_remote_copy(
            src_ref=src, dst_ref=dst, send_sem=ss, recv_sem=rs, device_id=dev, device_id_type=MESH
        )

    def send_ici(q, h):
        return remote(T.at[c, q], X.at[c, q], s_ici.at[q], r_ici.at[q], {"blk": nbr[h]})

    def send_core(q):
        return remote(T.at[c, q], T.at[c, q], s_core.at[q], r_core.at[q], {"col": 1 - c})

    def recv_core(q):
        return remote(T.at[c, q], T.at[1 - c, q], s_core.at[q], r_core.at[q], {"col": 1 - c})

    def send_fwd(q):
        return remote(X.at[c, q], X.at[c, q], s_fwd.at[q], r_fwd.at[q], {"col": 1 - c})

    def recv_fwd(q):
        return remote(X.at[c, q], X.at[1 - c, q], s_fwd.at[q], r_fwd.at[q], {"col": 1 - c})

    def send_p(q, h):
        return remote(X.at[1 - c, q], Precv.at[q], s_p.at[q], r_p.at[q], {"blk": nbr[1 - h]})

    def store_out(q):
        return pltpu.make_async_copy(T.at[1 - c, q], hbm_view(o_hbm, q), o_sem.at[q])

    def start_load(k):
        for h in range(2):
            load(h * half + k).start()

    def screen(k):
        for h in range(2):
            q = h * half + k
            load(q).wait()
            T[c, q] = T[c, q] * tm_ref[lax.rem(q, nl)]

    ahead = 2
    kept_dst = D.at[0, w] if spread else D
    inputs = [
        pltpu.make_async_copy(tmask_hbm, tmask_ref, in_sem.at[0]),
        pltpu.make_async_copy(dmask_hbm, dmask_ref, in_sem.at[1]),
        pltpu.make_async_copy(d_hbm, kept_dst, in_sem.at[2]),
    ]
    for copy in inputs:
        copy.start()
    for k in range(ahead):
        start_load(k)

    def spots(shape, axis, first):
        block = (lax.broadcasted_iota(jnp.int32, shape, axis) + first) // BS
        return (block == lax.broadcasted_iota(jnp.int32, shape, 1 - axis)).astype(jnp.float32)

    def expanded(mask_ref, flipped, rows, row0, columns, column0):
        mask = mask_ref[...].astype(jnp.float32)
        over, kept = (1, 0) if flipped else (0, 1)
        by_row = lax.dot_general(
            spots((rows, mask.shape[over]), 0, row0),
            mask,
            (((1,), (over,)), ((), ())),
            preferred_element_type=jnp.float32,
        )
        return jnp.dot(
            by_row, spots((mask.shape[kept], columns), 1, column0), preferred_element_type=jnp.float32
        )

    barrier = pltpu.get_barrier_semaphore()
    count = 3
    for h in range(2):
        pl.semaphore_signal(barrier, inc=1, device_id={"blk": nbr[h]}, device_id_type=MESH)
    pl.semaphore_signal(barrier, inc=1, device_id={"col": 1 - c}, device_id_type=MESH)
    if spread:
        for o in range(1, wide):
            pl.semaphore_signal(
                barrier, inc=1, device_id={"wide": lax.rem(w + o, wide)}, device_id_type=MESH
            )
        count += wide - 1
    for copy in inputs:
        copy.wait()
    if spread:
        rows, columns = d_hbm.shape
        D[0, w] = D[0, w] * expanded(dmask_ref, False, rows, g * rows, columns, w * columns)
    for j in range(nl):
        tm_ref[j] = expanded(tmask_ref, True, mu, g * mu, LANES, j * LANES)
    screen(0)
    pl.semaphore_wait(barrier, count)

    def need_own(m):
        return m != diag

    def need_0(m):
        return lax.rem(m, 2) == lax.rem(b, 2)

    def need_1(m):
        return m // 2 == b // 2

    needs = [need_own, need_0, need_1]

    def d_to_nbr(h):
        return remote(D.at[0, w], D.at[1 + h, w], s_dn.at[h], r_d.at[1 + h, w], {"blk": nbr[h]})

    def d_spread(r, o):
        dev = {"wide": lax.rem(w + o, wide)}
        return remote(D.at[r, w], D.at[r, w], s_dz.at[r, o], r_d.at[r, w], dev)

    def d_arrive(r, m):
        return remote(D.at[r, m], D.at[r, m], s_dz.at[r, 0], r_d.at[r, m], {"wide": lax.rem(w + 1, wide)})

    if spread:
        gives = [lax.rem(w, 2) != lax.rem(b, 2), w // 2 != b // 2]
        for h in range(2):
            @pl.when(gives[h])
            def _():
                d_to_nbr(h).start()

        @pl.when(need_own(w))
        def _():
            for o in range(1, wide):
                d_spread(0, o).start()

    def give(k):
        for h in range(2):
            q = h * half + k
            send_ici(q, h).start()
            send_core(q).start()

    def issue(k, _):
        start_load(k + ahead)
        give(k)
        screen(k + 1)
        return 0

    lax.fori_loop(0, half - ahead, issue, 0)
    give(half - 2)
    screen(half - 1)
    give(half - 1)

    if spread:
        for r in (1, 2):
            @pl.when(needs[r](w))
            def _():
                d_arrive(r, w).wait_recv()
                for o in range(1, wide):
                    d_spread(r, o).start()
        for r in range(3):
            for o in range(1, wide):
                m = lax.rem(w + o, wide)

                @pl.when(needs[r](m))
                def _():
                    d_arrive(r, m).wait_recv()

    kd = D.shape[3]
    for h in range(2):
        for i, r in enumerate((0, 2 - h)):
            for j, m in enumerate((b, nbr[h])):
                block = D[r, m]
                hi = block.astype(jnp.bfloat16)
                lo = (block - hi.astype(jnp.float32)).astype(jnp.bfloat16)
                DL[h, i * mu:(i + 1) * mu, j * kd:(j + 1) * kd] = hi
                DL[h, (2 + i) * mu:(3 + i) * mu, j * kd:(j + 1) * kd] = lo

    def forward(k):
        for h in range(2):
            q = h * half + k
            send_ici(q, h).wait_recv()
            send_fwd(q).start()

    def compute(k, _):
        forward(k)
        for h in range(2):
            q = h * half + k
            recv_core(q).wait_recv()
            recv_fwd(q).wait_recv()
            for i in range(4):
                piece = T[i, q] if i < 2 else X[i - 2, q]
                hi = piece.astype(jnp.bfloat16)
                th[i * mu:(i + 1) * mu] = hi
                tl[i * mu:(i + 1) * mu] = (piece - hi.astype(jnp.float32)).astype(jnp.bfloat16)
            first = jnp.dot(DL[h], th[...], preferred_element_type=jnp.float32)
            second = jnp.dot(DL[h, :2 * mu], tl[...], preferred_element_type=jnp.float32)
            total = first[:2 * mu] + first[2 * mu:] + second
            X[1 - c, q] = total[mu:]
            send_p(q, h).start()
            T[1 - c, q] = total[:mu]
        return 0

    lax.fori_loop(0, half, compute, 0)

    def finish(k, _):
        for h in range(2):
            q = h * half + k
            send_ici(q, h).wait_send()
            send_core(q).wait_send()
            send_fwd(q).wait_send()
            send_p(q, h).wait()
            T[1 - c, q] = T[1 - c, q] + Precv[q]
            store_out(q).start()
        return 0

    lax.fori_loop(0, half, finish, 0)

    def drain(k, _):
        for h in range(2):
            store_out(h * half + k).wait()
        return 0

    lax.fori_loop(0, half, drain, 0)

    if spread:
        for h in range(2):
            @pl.when(gives[h])
            def _():
                d_to_nbr(h).wait_send()
        for r in range(3):
            @pl.when(needs[r](w))
            def _():
                for o in range(1, wide):
                    d_spread(r, o).wait_send()


def on_device(tensor, density, tensor_mask, density_mask):
    wide, blk, col = (lax.axis_size(a) for a in ("wide", "blk", "col"))
    mu, ri, lam = tensor.shape
    nu, piece = density.shape
    nl = lam // LANES
    Q = ri * nl
    b, w = lax.axis_index("blk"), lax.axis_index("wide")
    g = b * col + lax.axis_index("col")
    kd = col * mu
    spread = piece == kd and wide == blk
    kept = density
    if not spread:
        dm = jnp.repeat(jnp.repeat(density_mask, BS, axis=0), BS, axis=1).astype(jnp.float32)
        kept = density * lax.dynamic_slice(dm, (g * nu, w * piece), (nu, piece))
        full = lax.all_gather(kept, "wide", axis=1, tiled=True)
        full = lax.all_gather(full, ("blk", "col"), axis=0, tiled=True)
        groups = [g, other_blk(b, 0) * col + lax.axis_index("col"), other_blk(b, 1) * col + lax.axis_index("col")]
        kept = jnp.stack(
            [lax.dynamic_slice_in_dim(full, i * nu, nu, 0).reshape(nu, blk, kd).transpose(1, 0, 2) for i in groups]
        )
    f32, bf16 = jnp.float32, jnp.bfloat16
    dma = pltpu.SemaphoreType.DMA
    flops = 2 * 2 * nu * 2 * kd * Q * LANES * 3
    return pl.pallas_call(
        functools.partial(kernel, spread, wide, ri, nl),
        out_shape=jax.ShapeDtypeStruct((mu, ri, lam), f32),
        in_specs=[
            pl.BlockSpec(memory_space=pltpu.HBM),
            pl.BlockSpec(memory_space=pltpu.HBM),
            pl.BlockSpec(memory_space=pltpu.HBM),
            pl.BlockSpec(memory_space=pltpu.HBM),
        ],
        out_specs=pl.BlockSpec(memory_space=pl.ANY),
        scratch_shapes=[
            pltpu.VMEM(tensor_mask.shape[::-1], jnp.int32),
            pltpu.VMEM(density_mask.shape, jnp.int32),
            pltpu.VMEM((nl, mu, LANES), f32),
            pltpu.VMEM((2, Q, mu, LANES), f32),
            pltpu.VMEM((2, Q, mu, LANES), f32),
            pltpu.VMEM((Q, nu, LANES), f32),
            pltpu.VMEM((3, blk, nu, kd), f32),
            pltpu.VMEM((2, 4 * nu, 2 * kd), bf16),
            pltpu.VMEM((2 * kd, LANES), bf16),
            pltpu.VMEM((2 * kd, LANES), bf16),
        ] + [dma((Q,))] * 10 + [dma((2,)), dma((3, wide)), dma((3, blk)), dma((3,))],
        compiler_params=pltpu.CompilerParams(
            collective_id=0, has_side_effects=True, vmem_limit_bytes=46 * 2**20
        ),
        cost_estimate=pl.CostEstimate(
            flops=flops, bytes_accessed=2 * mu * ri * lam * 4, transcendentals=0
        ),
    )(tensor, kept, tensor_mask.T, density_mask)


def solution(mesh):
    in_specs = (P(("blk", "col"), "wide", None), P(("blk", "col"), "wide"), P(), P())
    out_specs = P(("blk", "col"), "wide", None)
    return jax.shard_map(
        on_device, mesh=mesh, in_specs=in_specs, out_specs=out_specs, check_vma=False
    )
```

```python
import functools

import jax
import jax.numpy as jnp
from jax import lax
from jax.experimental import pallas as pl
from jax.experimental.pallas import tpu as pltpu
from jax.sharding import PartitionSpec as P

BS = 64
LANES = 512
MESH = pl.DeviceIdType.MESH


def other_blk(b, h):
    if h == 0:
        return b + 1 - 2 * lax.rem(b, 2)
    return lax.rem(b + 2, 4)


def kernel(
    spread, wide, ri, nl,
    t_hbm, d_hbm, tmask_hbm, dmask_hbm, o_hbm,
    tmask_ref, dmask_ref, tm_ref, T, X, Precv, D, DL, th, tl,
    load_sem, s_ici, r_ici, s_core, r_core, s_fwd, r_fwd, s_p, r_p, o_sem, s_dn, s_dz, r_d, in_sem,
):
    Q = ri * nl
    half = Q // 2
    mu = T.shape[2]
    b = lax.axis_index("blk")
    c = lax.axis_index("col")
    w = lax.axis_index("wide")
    g = b * 2 + c
    nbr = [other_blk(b, 0), other_blk(b, 1)]
    planes = [other_blk(w, 0), other_blk(w, 1)]
    planes.append(other_blk(planes[0], 1))

    def hbm_view(ref, q):
        return ref.at[:, q // nl, pl.ds(pl.multiple_of(lax.rem(q, nl) * LANES, LANES), LANES)]

    def load(q):
        return pltpu.make_async_copy(hbm_view(t_hbm, q), T.at[c, q], load_sem.at[q])

    def remote(src, dst, ss, rs, dev):
        return pltpu.make_async_remote_copy(
            src_ref=src, dst_ref=dst, send_sem=ss, recv_sem=rs, device_id=dev, device_id_type=MESH
        )

    def send_ici(q, h):
        return remote(T.at[c, q], X.at[c, q], s_ici.at[q], r_ici.at[q], {"blk": nbr[h]})

    def send_core(q):
        return remote(T.at[c, q], T.at[c, q], s_core.at[q], r_core.at[q], {"col": 1 - c})

    def recv_core(q):
        return remote(T.at[c, q], T.at[1 - c, q], s_core.at[q], r_core.at[q], {"col": 1 - c})

    def send_fwd(q):
        return remote(X.at[c, q], X.at[c, q], s_fwd.at[q], r_fwd.at[q], {"col": 1 - c})

    def recv_fwd(q):
        return remote(X.at[c, q], X.at[1 - c, q], s_fwd.at[q], r_fwd.at[q], {"col": 1 - c})

    def send_p(q, h):
        return remote(X.at[1 - c, q], Precv.at[q], s_p.at[q], r_p.at[q], {"blk": nbr[1 - h]})

    def store_out(q):
        return pltpu.make_async_copy(T.at[1 - c, q], hbm_view(o_hbm, q), o_sem.at[q])

    def start_load(k):
        for h in range(2):
            load(h * half + k).start()

    def screen(k):
        for h in range(2):
            q = h * half + k
            load(q).wait()
            T[c, q] = T[c, q] * tm_ref[lax.rem(q, nl)]

    ahead = 2
    kept_dst = D.at[0, w] if spread else D
    inputs = [
        pltpu.make_async_copy(tmask_hbm, tmask_ref, in_sem.at[0]),
        pltpu.make_async_copy(dmask_hbm, dmask_ref, in_sem.at[1]),
        pltpu.make_async_copy(d_hbm, kept_dst, in_sem.at[2]),
    ]
    for copy in inputs:
        copy.start()
    for k in range(ahead):
        start_load(k)

    def spots(shape, axis, first):
        block = (lax.broadcasted_iota(jnp.int32, shape, axis) + first) // BS
        return (block == lax.broadcasted_iota(jnp.int32, shape, 1 - axis)).astype(jnp.float32)

    def expanded(mask_ref, flipped, rows, row0, columns, column0):
        mask = mask_ref[...].astype(jnp.float32)
        over, kept = (1, 0) if flipped else (0, 1)
        by_row = lax.dot_general(
            spots((rows, mask.shape[over]), 0, row0),
            mask,
            (((1,), (over,)), ((), ())),
            preferred_element_type=jnp.float32,
        )
        return jnp.dot(
            by_row, spots((mask.shape[kept], columns), 1, column0), preferred_element_type=jnp.float32
        )

    barrier = pltpu.get_barrier_semaphore()
    count = 3
    for h in range(2):
        pl.semaphore_signal(barrier, inc=1, device_id={"blk": nbr[h]}, device_id_type=MESH)
    pl.semaphore_signal(barrier, inc=1, device_id={"col": 1 - c}, device_id_type=MESH)
    if spread:
        for plane in planes:
            pl.semaphore_signal(barrier, inc=1, device_id={"wide": plane}, device_id_type=MESH)
        count += wide - 1
    for copy in inputs:
        copy.wait()
    if spread:
        rows, columns = d_hbm.shape
        D[0, w] = D[0, w] * expanded(dmask_ref, False, rows, g * rows, columns, w * columns)
    for j in range(nl):
        tm_ref[j] = expanded(tmask_ref, True, mu, g * mu, LANES, j * LANES)
    screen(0)
    pl.semaphore_wait(barrier, count)

    part = D.shape[2] // 2
    bit = [lax.rem(b, 2), b // 2]

    def half_block(h, plane, wanted):
        if h == 0:
            return plane // 2 * 2 + wanted, lax.rem(plane + wanted, 2)
        return wanted * 2 + lax.rem(plane, 2), lax.rem(plane // 2 + wanted, 2)

    def d_view(r, h, plane, wanted):
        m, f = half_block(h, plane, wanted)
        return D.at[r, m, pl.ds(pl.multiple_of(f * part, part), part)]

    def d_own(i, plane=w):
        return remote(D.at[0, plane], D.at[0, plane], s_dz.at[0, i], r_d.at[0, plane], {"wide": planes[i]})

    def d_cross(h):
        return remote(
            d_view(0, h, w, 1 - bit[h]), d_view(1 + h, h, w, 1 - bit[h]),
            s_dn.at[h], r_d.at[1 + h, w], {"blk": nbr[h]},
        )

    def d_spread(h, i, plane=w):
        view = d_view(1 + h, h, plane, bit[h])
        return remote(view, view, s_dz.at[1 + h, i], r_d.at[1 + h, plane], {"wide": planes[i]})

    def is_late(h):
        return half_block(h, w, 1 - bit[h])[1] == 1

    if spread:
        for i in range(3):
            d_own(i).start()
        for h in range(2):
            @pl.when(jnp.logical_not(is_late(h)))
            def _():
                d_cross(h).start()

    def give(k):
        for h in range(2):
            q = h * half + k
            send_ici(q, h).start()
            send_core(q).start()

    def issue(k, _):
        start_load(k + ahead)
        give(k)
        screen(k + 1)
        return 0

    lax.fori_loop(0, 1, issue, 0)
    if spread:
        for h in range(2):
            @pl.when(is_late(h))
            def _():
                d_own(h, planes[h]).wait_recv()
                d_cross(h).start()
    lax.fori_loop(1, half - ahead, issue, 0)
    give(half - 2)
    screen(half - 1)
    give(half - 1)

    if spread:
        for h in range(2):
            d_spread(h, 0).wait_recv()
            for i in range(3):
                d_spread(h, i).start()
        for h in range(2):
            @pl.when(jnp.logical_not(is_late(h)))
            def _():
                d_own(h, planes[h]).wait_recv()
        d_own(2, planes[2]).wait_recv()
        for h in range(2):
            for i in range(3):
                d_spread(h, i, planes[i]).wait_recv()

    kd = D.shape[3]
    for h in range(2):
        for i, r in enumerate((0, 2 - h)):
            for j, m in enumerate((b, nbr[h])):
                block = D[r, m]
                hi = block.astype(jnp.bfloat16)
                lo = (block - hi.astype(jnp.float32)).astype(jnp.bfloat16)
                DL[h, i * mu:(i + 1) * mu, j * kd:(j + 1) * kd] = hi
                DL[h, (2 + i) * mu:(3 + i) * mu, j * kd:(j + 1) * kd] = lo

    def forward(k):
        for h in range(2):
            q = h * half + k
            send_ici(q, h).wait_recv()
            send_fwd(q).start()

    def compute(k, _):
        forward(k)
        for h in range(2):
            q = h * half + k
            recv_core(q).wait_recv()
            recv_fwd(q).wait_recv()
            for i in range(4):
                piece = T[i, q] if i < 2 else X[i - 2, q]
                hi = piece.astype(jnp.bfloat16)
                th[i * mu:(i + 1) * mu] = hi
                tl[i * mu:(i + 1) * mu] = (piece - hi.astype(jnp.float32)).astype(jnp.bfloat16)
            first = jnp.dot(DL[h], th[...], preferred_element_type=jnp.float32)
            second = jnp.dot(DL[h, :2 * mu], tl[...], preferred_element_type=jnp.float32)
            total = first[:2 * mu] + first[2 * mu:] + second
            X[1 - c, q] = total[mu:]
            send_p(q, h).start()
            T[1 - c, q] = total[:mu]
        return 0

    lax.fori_loop(0, half, compute, 0)

    def finish(k, _):
        for h in range(2):
            q = h * half + k
            send_ici(q, h).wait_send()
            send_core(q).wait_send()
            send_fwd(q).wait_send()
            send_p(q, h).wait()
            T[1 - c, q] = T[1 - c, q] + Precv[q]
            store_out(q).start()
        return 0

    lax.fori_loop(0, half, finish, 0)

    def drain(k, _):
        for h in range(2):
            store_out(h * half + k).wait()
        return 0

    lax.fori_loop(0, half, drain, 0)

    if spread:
        for i in range(3):
            d_own(i).wait_send()
        for h in range(2):
            d_cross(h).wait_send()
            for i in range(3):
                d_spread(h, i).wait_send()


def on_device(tensor, density, tensor_mask, density_mask):
    wide, blk, col = (lax.axis_size(a) for a in ("wide", "blk", "col"))
    mu, ri, lam = tensor.shape
    nu, piece = density.shape
    nl = lam // LANES
    Q = ri * nl
    b, w = lax.axis_index("blk"), lax.axis_index("wide")
    g = b * col + lax.axis_index("col")
    kd = col * mu
    spread = piece == kd and wide == blk == 4
    kept = density
    if not spread:
        dm = jnp.repeat(jnp.repeat(density_mask, BS, axis=0), BS, axis=1).astype(jnp.float32)
        kept = density * lax.dynamic_slice(dm, (g * nu, w * piece), (nu, piece))
        full = lax.all_gather(kept, "wide", axis=1, tiled=True)
        full = lax.all_gather(full, ("blk", "col"), axis=0, tiled=True)
        groups = [g, other_blk(b, 0) * col + lax.axis_index("col"), other_blk(b, 1) * col + lax.axis_index("col")]
        kept = jnp.stack(
            [lax.dynamic_slice_in_dim(full, i * nu, nu, 0).reshape(nu, blk, kd).transpose(1, 0, 2) for i in groups]
        )
    f32, bf16 = jnp.float32, jnp.bfloat16
    dma = pltpu.SemaphoreType.DMA
    flops = 2 * 2 * nu * 2 * kd * Q * LANES * 3
    return pl.pallas_call(
        functools.partial(kernel, spread, wide, ri, nl),
        out_shape=jax.ShapeDtypeStruct((mu, ri, lam), f32),
        in_specs=[
            pl.BlockSpec(memory_space=pltpu.HBM),
            pl.BlockSpec(memory_space=pltpu.HBM),
            pl.BlockSpec(memory_space=pltpu.HBM),
            pl.BlockSpec(memory_space=pltpu.HBM),
        ],
        out_specs=pl.BlockSpec(memory_space=pl.ANY),
        scratch_shapes=[
            pltpu.VMEM(tensor_mask.shape[::-1], jnp.int32),
            pltpu.VMEM(density_mask.shape, jnp.int32),
            pltpu.VMEM((nl, mu, LANES), f32),
            pltpu.VMEM((2, Q, mu, LANES), f32),
            pltpu.VMEM((2, Q, mu, LANES), f32),
            pltpu.VMEM((Q, nu, LANES), f32),
            pltpu.VMEM((3, blk, nu, kd), f32),
            pltpu.VMEM((2, 4 * nu, 2 * kd), bf16),
            pltpu.VMEM((2 * kd, LANES), bf16),
            pltpu.VMEM((2 * kd, LANES), bf16),
        ] + [dma((Q,))] * 10 + [dma((2,)), dma((3, 3)), dma((3, blk)), dma((3,))],
        compiler_params=pltpu.CompilerParams(
            collective_id=0, has_side_effects=True, vmem_limit_bytes=46 * 2**20
        ),
        cost_estimate=pl.CostEstimate(
            flops=flops, bytes_accessed=2 * mu * ri * lam * 4, transcendentals=0
        ),
    )(tensor, kept, tensor_mask.T, density_mask)


def solution(mesh):
    in_specs = (P(("blk", "col"), "wide", None), P(("blk", "col"), "wide"), P(), P())
    out_specs = P(("blk", "col"), "wide", None)
    return jax.shard_map(
        on_device, mesh=mesh, in_specs=in_specs, out_specs=out_specs, check_vma=False
    )
```
